32 devices in a mesh: pb: 8 (over y, x, core), row: 4 (over z).
Axes of the slice: x: 2, y: 2, z: 4, core: 2. Of those that a mesh axis runs over, the one named last changes fastest.
Arguments:
- query_emb: bfloat16 [16384, 512], P(('pb', 'row')), may hold values from -4 to 4
- query_scales: float32 [16384, 4], P(('pb', 'row')), may hold values from 0.25 to 4
- sharpness: float32 [16384], P(('pb', 'row')), may hold values from 4 to 400
- ref_emb: bfloat16 [32768, 512], P(('pb', 'row')), may hold values from -4 to 4
- ref_scales: float32 [32768, 4], P(('pb', 'row')), may hold values from 0.25 to 4
- properties: bfloat16 [32768, 128], P(('pb', 'row')), may hold values from -4 to 4
- band_mask: int32 [64, 128], P(('pb', 'row')), may hold values from 0 to 1, as said below
- ref_skew: int32 [8], replicated, may hold values from 0 to 3, as said below
Outputs:
- transferred: float32 [16384, 128], P(('pb', 'row'))
The draws below stay inside these ranges and needn't reach their ends.
Inputs may be any that keep to these rules, and one draw needn't show every extreme that they name: `band_mask`: for k = p * 4 + r, every tile of query rows of block k has a 1 against some tile of reference block p * 4 + ((r - ref_skew[p]) mod 4). `ref_skew`: every value from 0 to 3 occurs.
All inputs are finite; a program needn't handle non-finite values.
Results may differ from the reference program's by a relative error of at most 0.007.
Values may be sent and summed in bfloat16 or wider, within the bound.
A program may use at most 64 MiB of HBM per device.

```python
import math
import jax
import jax.numpy as jnp
from jax import lax

E = 512
PROPS = 128
SCALE_BLOCK = 128
TILE = 256
STEPS = 4
QB = 512
RB = 1024
NQ = 16384
NR = 32768
N_PB = 8
N_ROW = 4


def skew_table(key):
    return (jax.random.permutation(jax.random.fold_in(key, 3), N_PB) % N_ROW).astype(jnp.int32)


def first_visits(key):
    offsets = skew_table(key)
    blocks = jnp.arange(N_PB * N_ROW, dtype=jnp.int32)
    home_pb = blocks // N_ROW
    home_row = blocks % N_ROW
    return home_pb * N_ROW + (home_row - offsets[home_pb]) % N_ROW


def reference_rows(key):
    values = jnp.clip(jax.random.normal(jax.random.fold_in(key, 101), (NR, E), jnp.float32), -4.0, 4.0)
    return values


def reference_scale_rows(key):
    groups = E // SCALE_BLOCK
    values = jnp.exp(jax.random.uniform(jax.random.fold_in(key, 111), (NR, groups), jnp.float32, math.log(0.5), math.log(2.0)))
    return values


def draw_ref_emb(key, part):
    return reference_rows(key).astype(jnp.bfloat16)


def draw_ref_scales(key, part):
    return reference_scale_rows(key)


def draw_query_emb(key, part):
    values = jnp.clip(jax.random.normal(jax.random.fold_in(key, 201), (NQ, E), jnp.float32), -4.0, 4.0)
    return values.astype(jnp.bfloat16)


def draw_query_scales(key, part):
    groups = E // SCALE_BLOCK
    values = jnp.exp(jax.random.uniform(jax.random.fold_in(key, 211), (NQ, groups), jnp.float32, math.log(0.5), math.log(2.0)))
    return values


def draw_sharpness(key, part):
    values = jnp.exp(jax.random.uniform(jax.random.fold_in(key, 221), (NQ,), jnp.float32, math.log(4.0), math.log(64.0)))
    return values


def draw_ref_skew(key, part):
    return skew_table(key)


def draw_band_mask(key, part):
    query_bands = jax.random.randint(jax.random.fold_in(key, 301), (NQ // TILE,), 0, 8)
    ref_bands = jax.random.randint(jax.random.fold_in(key, 302), (NR // TILE,), 0, 8)
    allowed = (jnp.abs(query_bands[:, None] - ref_bands[None, :]) <= 1).astype(jnp.int32)
    query_tiles = QB // TILE
    ref_tiles = RB // TILE
    tiles = jnp.arange(NQ // TILE, dtype=jnp.int32)
    columns = first_visits(key)[tiles // query_tiles] * ref_tiles + tiles % query_tiles % ref_tiles
    return allowed.at[tiles, columns].set(1)


def levels(key, dims, pieces, low, top_value):
    def one(dim, blocks):
        heights = jax.random.uniform(jax.random.fold_in(jax.random.fold_in(key, 6), dim), (blocks,), jnp.float32, low / len(pieces), top_value / len(pieces))
        return jnp.repeat(jnp.exp(heights), dims[dim] // blocks).reshape((-1,) + (1,) * (len(dims) - dim - 1))

    factor_of = one(*pieces[0])
    for cut in pieces[1:]:
        factor_of = factor_of * one(*cut)
    return factor_of


def gaussian(key, dims, width, bound, shards=(), held_as=jnp.bfloat16):
    entries = jax.random.normal(key, dims, jnp.float32) * width
    if len(shards) > 0:
        entries = levels(key, dims, shards, -0.22, 0.18) * entries
    return jnp.clip(entries, min=-bound, max=bound).astype(held_as)


def setup_inputs(seed: int = 0) -> dict:
    arg_keys = jax.random.split(jax.random.key(seed), 9)
    query_emb = draw_query_emb(jax.random.fold_in(arg_keys[8], 71), 0)
    query_scales = draw_query_scales(jax.random.fold_in(arg_keys[8], 71), 0)
    sharpness = draw_sharpness(jax.random.fold_in(arg_keys[8], 71), 0)
    ref_emb = draw_ref_emb(jax.random.fold_in(arg_keys[8], 71), 0)
    ref_scales = draw_ref_scales(jax.random.fold_in(arg_keys[8], 71), 0)
    properties = gaussian(arg_keys[5], (NR, PROPS), 1.0, 4.0, ((0, 32),))
    band_mask = draw_band_mask(jax.random.fold_in(arg_keys[8], 71), 0)
    ref_skew = draw_ref_skew(jax.random.fold_in(arg_keys[8], 71), 0)
    return {"query_emb": query_emb, "query_scales": query_scales, "sharpness": sharpness, "ref_emb": ref_emb, "ref_scales": ref_scales, "properties": properties, "band_mask": band_mask, "ref_skew": ref_skew}


EPSILON = 1e-6
FLOOR = -1e30


def dequantize(values, scales):
    row_count, column_count = values.shape
    groups = scales.shape[1]
    widened = values.astype(jnp.float32).reshape(row_count, groups, column_count // groups) * scales[:, :, None]
    return widened.reshape(row_count, column_count).astype(jnp.bfloat16)


def squares(matrix):
    return jnp.sum(jnp.square(matrix.astype(jnp.float32)), axis=1)


def visit(carried, queries, query_sq, sharpen, references, props, counted_tiles, tile_rows):
    run_max, run_sum, weighted = carried
    reference_sq = squares(references)
    products = lax.dot_general(queries, references, (((1,), (1,)), ((), ())), preferred_element_type=jnp.float32)
    scores = sharpen[:, None] * products / (query_sq[:, None] + reference_sq[None, :] - products + EPSILON)
    query_tiles, ref_tiles = counted_tiles.shape
    counted = jnp.broadcast_to(counted_tiles[:, None, :, None], (query_tiles, tile_rows, ref_tiles, tile_rows))
    counted = counted.reshape(query_tiles * tile_rows, ref_tiles * tile_rows)
    new_max = jnp.maximum(run_max, jnp.max(jnp.where(counted, scores, FLOOR), axis=1))
    rescale = jnp.exp(run_max - new_max)
    weights = jnp.where(counted, jnp.exp(scores - new_max[:, None]), 0.0)
    run_sum = rescale * run_sum + jnp.sum(weights, axis=1)
    weighted = rescale[:, None] * weighted + jnp.dot(weights.astype(jnp.bfloat16), props, preferred_element_type=jnp.float32)
    return new_max, run_sum, weighted


def reference(query_emb, query_scales, sharpness, ref_emb, ref_scales, properties, band_mask, ref_skew):
    queries = dequantize(query_emb, query_scales)
    query_sq = squares(queries)
    references = dequantize(ref_emb, ref_scales)
    query_tiles = QB // TILE
    ref_tiles = RB // TILE

    def one_block(block_index):
        home_pb = block_index // N_ROW
        home_row = block_index % N_ROW
        own_rows = lax.dynamic_slice_in_dim(queries, block_index * QB, QB, 0)
        own_sq = lax.dynamic_slice_in_dim(query_sq, block_index * QB, QB, 0)
        own_sharpen = lax.dynamic_slice_in_dim(sharpness, block_index * QB, QB, 0)
        carried = (jnp.full((QB,), FLOOR, jnp.float32), jnp.zeros((QB,), jnp.float32), jnp.zeros((QB, PROPS), jnp.float32))
        for turn_index in range(STEPS):
            pb_group = (home_pb + turn_index) % N_PB
            row_slot = (home_row - ref_skew[pb_group] - turn_index) % N_ROW
            visited = (pb_group * N_ROW + row_slot).astype(jnp.int32)
            block_refs = lax.dynamic_slice_in_dim(references, visited * RB, RB, 0)
            block_props = lax.dynamic_slice_in_dim(properties, visited * RB, RB, 0)
            counted_tiles = lax.dynamic_slice(band_mask, (block_index * query_tiles, visited * ref_tiles), (query_tiles, ref_tiles)) == 1
            carried = visit(carried, own_rows, own_sq, own_sharpen, block_refs, block_props, counted_tiles, TILE)
        return carried[2] / carried[1][:, None]

    result = lax.map(one_block, jnp.arange(N_PB * N_ROW, dtype=jnp.int32))
    return result.reshape(N_PB * N_ROW * QB, PROPS)
```

```python
import functools

import jax
import jax.numpy as jnp
from jax import lax
from jax.experimental import pallas as pl
from jax.experimental.pallas import tpu as pltpu
from jax.sharding import PartitionSpec as P

STEPS = 4
CHUNKS = 4
REF_PIECE = 256
STAT_ROWS = 16
EPSILON = 1e-06
FLOOR = -1e30
LOW = -1e29
MESH = pl.DeviceIdType.MESH
NT = (((1,), (1,)), ((), ()))


def dequantize(values, scales):
    groups = scales.shape[1]
    width = values.shape[1] // groups
    wide = values.astype(jnp.float32)
    parts = [
        (wide[:, g * width : (g + 1) * width] * scales[:, g : g + 1]).astype(jnp.bfloat16)
        for g in range(groups)
    ]
    return jnp.concatenate(parts, axis=1)


def split_squares(matrix):
    square = jnp.square(matrix.astype(jnp.float32))
    high = square.astype(jnp.bfloat16)
    return high, (square - high.astype(jnp.float32)).astype(jnp.bfloat16)


def split_three(value):
    high = value.astype(jnp.bfloat16).astype(jnp.float32)
    rest = value - high
    middle = rest.astype(jnp.bfloat16).astype(jnp.float32)
    return [high, middle, rest - middle]


def kernel(
    n_pb,
    n_row,
    query_emb,
    query_scales,
    sharpness,
    ref_emb,
    ref_scales,
    properties,
    band_mask,
    ref_skew,
    out,
    refs,
    ref_sq,
    props_t,
    scores,
    aux_own,
    aux_in,
    aux_stage,
    aux_z,
    aux_x_send,
    aux_x_recv,
    aux_z_send,
    aux_z_recv,
    x_send,
    x_recv,
    z_send,
    z_recv,
    rz_send,
    rz_recv,
    rx_send,
    rx_recv,
    *buffers,
):
    place = lax.axis_index("pb")
    slot = lax.axis_index("row")
    chunks = CHUNKS
    queries_in = buffers[0:chunks]
    queries_stage = buffers[chunks : 2 * chunks]
    queries_z = buffers[2 * chunks : 3 * chunks]
    made = buffers[3 * chunks : 4 * chunks]
    returned = buffers[4 * chunks : 5 * chunks]
    passed = buffers[5 * chunks : 6 * chunks]
    finished = buffers[6 * chunks : 7 * chunks]

    query_total, width = query_emb.shape
    ref_total = ref_emb.shape[0]
    rows = query_total // chunks
    tile_rows = query_total // band_mask.shape[0]
    query_tiles = query_total // tile_rows
    ref_tiles = ref_total // tile_rows
    prop_width = properties.shape[1]

    def at_pb(steps):
        return (lax.rem(place + n_pb + steps, n_pb), slot)

    def at_row(steps):
        return (place, lax.rem(slot + n_row + steps, n_row))

    partners = [at_pb(t) for t in range(1, STEPS)] + [at_pb(-t) for t in range(1, STEPS)]
    partners += [at_row(d) for d in range(1, n_row)]
    barrier = pltpu.get_barrier_semaphore()
    for partner in partners:
        pl.semaphore_signal(barrier, inc=1, device_id=partner, device_id_type=MESH)

    def remote(source, target, send, recv, device):
        return pltpu.make_async_remote_copy(
            src_ref=source,
            dst_ref=target,
            send_sem=send,
            recv_sem=recv,
            device_id=device,
            device_id_type=MESH,
        )

    def aux_x(t):
        return remote(
            aux_own.at[t], aux_in.at[t], aux_x_send.at[t], aux_x_recv.at[t], at_pb(t)
        )

    def aux_to_z(d):
        return remote(
            aux_stage.at[d], aux_z.at[d], aux_z_send.at[d], aux_z_recv.at[d], at_row(d)
        )

    def go_x(c, t):
        k = c * STEPS + t
        return remote(
            queries_in[c].at[0], queries_in[c].at[t], x_send.at[k], x_recv.at[k], at_pb(t)
        )

    def go_z(c, d):
        k = c * n_row + d
        return remote(
            queries_stage[c].at[d], queries_z[c].at[d], z_send.at[k], z_recv.at[k], at_row(d)
        )

    def back_z(c, d):
        k = c * n_row + d
        return remote(
            made[c].at[d], returned[c].at[d], rz_send.at[k], rz_recv.at[k], at_row(-d)
        )

    def back_x(c, t):
        k = c * STEPS + t
        return remote(
            passed[c].at[t], finished[c].at[t], rx_send.at[k], rx_recv.at[k], at_pb(-t)
        )

    own_skew = ref_skew[place]

    def turned(steps):
        return lax.rem(2 * n_row - steps - own_skew, n_row)

    def visit_of(d):
        return jnp.minimum(turned(d), STEPS - 1)

    ones = jnp.ones((8, width), jnp.bfloat16)
    for c in range(chunks):
        part = pl.ds(c * rows, rows)
        queries_in[c][0] = dequantize(query_emb[part, :], query_scales[part, :])
        if c == 0:
            pl.semaphore_wait(barrier, len(partners))
        for t in range(STEPS - 1, 0, -1):
            go_x(c, t).start()
    lanes = lax.broadcasted_iota(jnp.int32, (1, query_total), 1) // tile_rows
    squares = []
    for c in range(chunks):
        high, low = split_squares(queries_in[c][0])
        squares.append(
            (
                lax.dot_general(ones, high, NT, preferred_element_type=jnp.float32)
                + lax.dot_general(ones, low, NT, preferred_element_type=jnp.float32)
            )[0:1]
        )
    query_sq = jnp.concatenate(squares, axis=1)
    for t in range(STEPS):
        group = lax.rem(place + t, n_pb)
        row_slot = lax.rem(slot - ref_skew[group] - t + 8 * n_row, n_row)
        first = (group * n_row + row_slot) * ref_tiles
        lines = [sharpness[...], query_sq]
        for j in range(ref_tiles):
            line = jnp.zeros((1, query_total), jnp.float32)
            for i in range(query_tiles):
                bias = jnp.where(band_mask[i, first + j] == 1, 0.0, FLOOR)
                line = jnp.where(lanes == i, bias, line)
            lines.append(line)
        lines.append(jnp.zeros((8 - len(lines), query_total), jnp.float32))
        (aux_in.at[0] if t == 0 else aux_own.at[t])[...] = jnp.concatenate(lines, axis=0)
        if t > 0:
            aux_x(t).start()

    ones_ref = jnp.ones((rows, width), jnp.bfloat16)

    def prepare(i, _):
        part = pl.ds(pl.multiple_of(i * REF_PIECE, REF_PIECE), REF_PIECE)
        block = dequantize(ref_emb[part, :], ref_scales[part, :])
        refs[part, :] = block
        high, low = split_squares(block)
        ref_sq[part, :] = (
            lax.dot_general(high, ones_ref, NT, preferred_element_type=jnp.float32)
            + lax.dot_general(low, ones_ref, NT, preferred_element_type=jnp.float32)
            + EPSILON
        )
        return 0

    lax.fori_loop(0, ref_total // REF_PIECE, prepare, 0)
    for j in range(ref_total // REF_PIECE):
        part = pl.ds(j * REF_PIECE, REF_PIECE)
        props_t[:, part] = properties[part, :].astype(jnp.float32).T.astype(jnp.bfloat16)

    def distribute(c):
        if c == 0:
            for t in range(1, STEPS):
                aux_x(t).wait_recv()
            for d in range(1, n_row):
                aux_stage[d] = aux_in[visit_of(d)]
                aux_to_z(d).start()
            aux_z[0] = aux_in[visit_of(0)]
        for t in range(1, STEPS):
            go_x(c, t).wait_recv()
        for d in range(1, n_row):
            queries_stage[c][d] = queries_in[c][visit_of(d)]
            go_z(c, d).start()
        queries_z[c][0] = queries_in[c][visit_of(0)]

    def attend(c, d):
        queries = queries_z[c][d]
        columns = slice(c * rows, (c + 1) * rows)
        sharpen = aux_z[d, 0:1, columns]
        own_sq = aux_z[d, 1:2, columns]
        top = jnp.full((1, rows), LOW, jnp.float32)
        for j in range(ref_tiles):
            part = slice(j * tile_rows, (j + 1) * tile_rows)
            inner = lax.dot_general(
                refs[part, :], queries, NT, preferred_element_type=jnp.float32
            )
            score = sharpen * inner / (ref_sq[part, :] + own_sq - inner)
            score = score + aux_z[d, 2 + j : 3 + j, columns]
            scores[part, :] = score
            top = jnp.maximum(top, jnp.max(score, axis=0, keepdims=True))
        total = jnp.zeros((1, rows), jnp.float32)
        weighted = jnp.zeros((prop_width, rows), jnp.float32)
        for j in range(ref_tiles):
            part = slice(j * tile_rows, (j + 1) * tile_rows)
            weights = jnp.exp(scores[part, :] - top)
            total = total + jnp.sum(weights, axis=0, keepdims=True)
            weighted = weighted + jnp.dot(
                props_t[:, part], weights.astype(jnp.bfloat16), preferred_element_type=jnp.float32
            )
        stats = split_three(top) + split_three(total)
        stats.append(jnp.zeros((STAT_ROWS - len(stats), rows), jnp.float32))
        return weighted.astype(jnp.bfloat16), jnp.concatenate(stats, axis=0).astype(jnp.bfloat16)

    def work(c):
        if c == 0:
            for d in range(1, n_row):
                aux_to_z(d).wait_recv()

        def one(d, _):
            @pl.when(d > 0)
            def _():
                go_z(c, d).wait_recv()

            weighted, stats = attend(c, d)
            made[c][d, 0:prop_width, :] = weighted
            made[c][d, prop_width:, :] = stats

            @pl.when(d > 0)
            def _():
                back_z(c, d).start()

            return 0

        lax.fori_loop(0, n_row, one, 0)
        returned[c][0] = made[c][0]

    def collect(c):
        for d in range(1, n_row):
            back_z(c, d).wait_recv()
        for t in range(STEPS - 1, 0, -1):
            passed[c][t] = returned[c][turned(t)]
            back_x(c, t).start()
        finished[c][0] = returned[c][turned(0)]

    def finish(c):
        for t in range(1, STEPS):
            back_x(c, t).wait_recv()
        tops, totals = [], []
        for t in range(STEPS):
            stats = finished[c][t, prop_width:, :].astype(jnp.float32)
            tops.append(stats[0:1] + stats[1:2] + stats[2:3])
            totals.append(stats[3:4] + stats[4:5] + stats[5:6])
        top = functools.reduce(jnp.maximum, tops)
        total = jnp.zeros((1, rows), jnp.float32)
        weighted = jnp.zeros((prop_width, rows), jnp.float32)
        for t in range(STEPS):
            rescale = jnp.exp(tops[t] - top)
            total = total + rescale * totals[t]
            weighted = weighted + rescale * finished[c][t, 0:prop_width, :].astype(jnp.float32)
        out[c * rows : (c + 1) * rows, :] = (weighted / total).T

    for step in range(chunks + 3):
        if step < chunks:
            distribute(step)
        if 0 <= step - 1 < chunks:
            work(step - 1)
        if 0 <= step - 2 < chunks:
            collect(step - 2)
        if 0 <= step - 3 < chunks:
            finish(step - 3)

    for t in range(1, STEPS):
        aux_x(t).wait_send()
    for d in range(1, n_row):
        aux_to_z(d).wait_send()
    for c in range(chunks):
        for t in range(1, STEPS):
            go_x(c, t).wait_send()
            back_x(c, t).wait_send()
        for d in range(1, n_row):
            go_z(c, d).wait_send()
            back_z(c, d).wait_send()


def local(query_emb, query_scales, sharpness, ref_emb, ref_scales, properties, band_mask, ref_skew):
    n_pb = lax.axis_size("pb")
    n_row = lax.axis_size("row")
    query_total, width = query_emb.shape
    ref_total = ref_emb.shape[0]
    prop_width = properties.shape[1]
    rows = query_total // CHUNKS
    low = jnp.bfloat16
    packed = (prop_width + STAT_ROWS, rows)
    kinds = [
        (STEPS, rows, width),
        (n_row, rows, width),
        (n_row, rows, width),
        (n_row,) + packed,
        (n_row,) + packed,
        (STEPS,) + packed,
        (STEPS,) + packed,
    ]
    vmem = pl.BlockSpec(memory_space=pltpu.VMEM)
    smem = pl.BlockSpec(memory_space=pltpu.SMEM)
    dma = pltpu.SemaphoreType.DMA
    sems = [STEPS, STEPS, n_row, n_row]
    sems += [CHUNKS * STEPS] * 2 + [CHUNKS * n_row] * 4 + [CHUNKS * STEPS] * 2
    pairs = STEPS * query_total * ref_total
    return pl.pallas_call(
        functools.partial(kernel, n_pb, n_row),
        out_shape=jax.ShapeDtypeStruct((query_total, prop_width), jnp.float32),
        in_specs=[vmem] * 6 + [smem] * 2,
        out_specs=vmem,
        scratch_shapes=[
            pltpu.VMEM((ref_total, width), low),
            pltpu.VMEM((ref_total, rows), jnp.float32),
            pltpu.VMEM((prop_width, ref_total), low),
            pltpu.VMEM((ref_total, rows), jnp.float32),
            pltpu.VMEM((STEPS, 8, query_total), jnp.float32),
            pltpu.VMEM((STEPS, 8, query_total), jnp.float32),
            pltpu.VMEM((n_row, 8, query_total), jnp.float32),
            pltpu.VMEM((n_row, 8, query_total), jnp.float32),
        ]
        + [dma((count,)) for count in sems]
        + [pltpu.VMEM(kind, low) for kind in kinds for _ in range(CHUNKS)],
        compiler_params=pltpu.CompilerParams(
            collective_id=0, has_side_effects=True, vmem_limit_bytes=56 * 1024 * 1024
        ),
        cost_estimate=pl.CostEstimate(
            flops=2 * pairs * (width + prop_width),
            bytes_accessed=4 * 1024 * 1024,
            transcendentals=2 * pairs,
        ),
    )(
        query_emb,
        query_scales,
        sharpness.reshape(1, query_total),
        ref_emb,
        ref_scales,
        properties,
        band_mask,
        ref_skew,
    )


def solution(mesh):
    placed = (
        P(("pb", "row"), None),
        P(("pb", "row"), None),
        P(("pb", "row")),
        P(("pb", "row"), None),
        P(("pb", "row"), None),
        P(("pb", "row"), None),
        P(("pb", "row"), None),
        P(),
    )
    return jax.shard_map(
        local, mesh=mesh, in_specs=placed, out_specs=P(("pb", "row"), None), check_vma=False
    )
```

```python
import functools

import jax
import jax.numpy as jnp
from jax import lax
from jax.experimental import pallas as pl
from jax.experimental.pallas import tpu as pltpu
from jax.sharding import PartitionSpec as P

STEPS = 4
CHUNKS = 4
REF_PIECE = 256
STAT_ROWS = 16
EPSILON = 1e-06
FLOOR = -1e30
LOW = -1e29
MESH = pl.DeviceIdType.MESH
NT = (((1,), (1,)), ((), ()))


def dequantize(values, scales):
    groups = scales.shape[0]
    scales = jnp.concatenate([scales, jnp.zeros((8 - groups, scales.shape[1]), jnp.float32)], axis=0).T
    width = values.shape[1] // groups
    wide = values.astype(jnp.float32)
    parts = [
        (wide[:, g * width : (g + 1) * width] * scales[:, g : g + 1]).astype(jnp.bfloat16)
        for g in range(groups)
    ]
    return jnp.concatenate(parts, axis=1)


def split_squares(matrix):
    square = jnp.square(matrix.astype(jnp.float32))
    high = square.astype(jnp.bfloat16)
    return high, (square - high.astype(jnp.float32)).astype(jnp.bfloat16)


def split_three(value):
    high = value.astype(jnp.bfloat16).astype(jnp.float32)
    rest = value - high
    middle = rest.astype(jnp.bfloat16).astype(jnp.float32)
    return [high, middle, rest - middle]


def kernel(
    n_pb,
    n_row,
    query_emb,
    query_scales,
    sharpness,
    ref_emb,
    ref_scales,
    properties,
    band_mask,
    ref_skew,
    out,
    refs,
    ref_sq,
    props_t,
    scores,
    aux_own,
    aux_in,
    aux_stage,
    aux_z,
    aux_x_send,
    aux_x_recv,
    aux_z_send,
    aux_z_recv,
    x_send,
    x_recv,
    up_send,
    up_recv,
    down_send,
    down_recv,
    rz_send,
    rz_recv,
    rx_send,
    rx_recv,
    *buffers,
):
    place = lax.axis_index("pb")
    slot = lax.axis_index("row")
    chunks = CHUNKS
    gathered = buffers[0:chunks]
    queries_stage = buffers[chunks : 2 * chunks]
    queries_in = buffers[2 * chunks : 3 * chunks]
    made = buffers[3 * chunks : 4 * chunks]
    returned = buffers[4 * chunks : 5 * chunks]
    passed = buffers[5 * chunks : 6 * chunks]
    finished = buffers[6 * chunks : 7 * chunks]

    query_total, width = query_emb.shape
    ref_total = ref_emb.shape[0]
    rows = query_total // chunks
    tile_rows = query_total // band_mask.shape[0]
    query_tiles = query_total // tile_rows
    ref_tiles = ref_total // tile_rows
    prop_width = properties.shape[1]

    def at_pb(steps):
        return (lax.rem(place + n_pb + steps, n_pb), slot)

    def at_row(steps):
        return (place, lax.rem(slot + n_row + steps, n_row))

    partners = [at_pb(t) for t in range(1, STEPS)] + [at_pb(-t) for t in range(1, STEPS)]
    partners += [at_row(d) for d in range(1, n_row)]
    barrier = pltpu.get_barrier_semaphore()
    for partner in partners:
        pl.semaphore_signal(barrier, inc=1, device_id=partner, device_id_type=MESH)

    def remote(source, target, send, recv, device):
        return pltpu.make_async_remote_copy(
            src_ref=source,
            dst_ref=target,
            send_sem=send,
            recv_sem=recv,
            device_id=device,
            device_id_type=MESH,
        )

    def aux_x(t):
        return remote(
            aux_own.at[t], aux_in.at[t], aux_x_send.at[t], aux_x_recv.at[t], at_pb(t)
        )

    def aux_to_z(d):
        return remote(
            aux_stage.at[d], aux_z.at[d], aux_z_send.at[d], aux_z_recv.at[d], at_row(d)
        )

    def go_x(c, t):
        k = c * STEPS + t
        return remote(
            queries_stage[c].at[t], queries_in[c].at[t], x_send.at[k], x_recv.at[k], at_pb(t)
        )

    def go_up(c, h):
        block = gathered[c].at[lax.rem(slot + n_row - h, n_row)]
        k = c * n_row + h
        return remote(block, block, up_send.at[k], up_recv.at[k], at_row(1))

    def go_down(c, h):
        block = gathered[c].at[lax.rem(slot + h, n_row)]
        k = c * n_row + h
        return remote(block, block, down_send.at[k], down_recv.at[k], at_row(-1))

    def from_below(c, h):
        block = gathered[c].at[lax.rem(slot + n_row - h, n_row)]
        k = c * n_row + h - 1
        return remote(block, block, up_send.at[k], up_recv.at[k], at_row(1))

    def from_above(c, h):
        block = gathered[c].at[lax.rem(slot + h, n_row)]
        k = c * n_row + h - 1
        return remote(block, block, down_send.at[k], down_recv.at[k], at_row(-1))

    def hop(c, h):
        @pl.when(slot >= h)
        def _():
            if h > 0:
                from_below(c, h).wait_recv()

            @pl.when(slot < n_row - 1)
            def _():
                go_up(c, h).start()

        @pl.when(slot + h < n_row)
        def _():
            if h > 0:
                from_above(c, h).wait_recv()

            @pl.when(slot > 0)
            def _():
                go_down(c, h).start()

    def sent(c, h):
        @pl.when((slot >= h) & (slot < n_row - 1))
        def _():
            go_up(c, h).wait_send()

        @pl.when((slot + h < n_row) & (slot > 0))
        def _():
            go_down(c, h).wait_send()

    def back_z(c, d):
        k = c * n_row + d
        return remote(
            made[c].at[d], returned[c].at[d], rz_send.at[k], rz_recv.at[k], at_row(-d)
        )

    def back_x(c, t):
        k = c * STEPS + t
        return remote(
            passed[c].at[t], finished[c].at[t], rx_send.at[k], rx_recv.at[k], at_pb(-t)
        )

    own_skew = ref_skew[place]

    def turned(steps):
        return lax.rem(2 * n_row - steps - own_skew, n_row)

    def visit_of(d):
        return jnp.minimum(turned(d), STEPS - 1)

    ones = jnp.ones((8, width), jnp.bfloat16)
    for c in range(chunks):
        part = pl.ds(c * rows, rows)
        gathered[c][slot] = dequantize(query_emb[part, :], query_scales[:, part])
        if c == 0:
            pl.semaphore_wait(barrier, len(partners))
            hop(0, 0)
    lanes = lax.broadcasted_iota(jnp.int32, (1, query_total), 1) // tile_rows
    squares = []
    for c in range(chunks):
        high, low = split_squares(gathered[c][slot])
        squares.append(
            (
                lax.dot_general(ones, high, NT, preferred_element_type=jnp.float32)
                + lax.dot_general(ones, low, NT, preferred_element_type=jnp.float32)
            )[0:1]
        )
    query_sq = jnp.concatenate(squares, axis=1)
    for t in range(STEPS):
        group = lax.rem(place + t, n_pb)
        row_slot = lax.rem(slot - ref_skew[group] - t + 8 * n_row, n_row)
        first = (group * n_row + row_slot) * ref_tiles
        lines = [sharpness[...], query_sq]
        for j in range(ref_tiles):
            line = jnp.zeros((1, query_total), jnp.float32)
            for i in range(query_tiles):
                bias = jnp.where(band_mask[i, first + j] == 1, 0.0, FLOOR)
                line = jnp.where(lanes == i, bias, line)
            lines.append(line)
        lines.append(jnp.zeros((8 - len(lines), query_total), jnp.float32))
        (aux_in.at[0] if t == 0 else aux_own.at[t])[...] = jnp.concatenate(lines, axis=0)
        if t > 0:
            aux_x(t).start()

    ones_ref = jnp.ones((rows, width), jnp.bfloat16)

    def prepare(i, _):
        part = pl.ds(pl.multiple_of(i * REF_PIECE, REF_PIECE), REF_PIECE)
        block = dequantize(ref_emb[part, :], ref_scales[:, part])
        refs[part, :] = block
        high, low = split_squares(block)
        ref_sq[part, :] = (
            lax.dot_general(high, ones_ref, NT, preferred_element_type=jnp.float32)
            + lax.dot_general(low, ones_ref, NT, preferred_element_type=jnp.float32)
            + EPSILON
        )
        return 0

    lax.fori_loop(0, ref_total // REF_PIECE, prepare, 0)
    for j in range(ref_total // REF_PIECE):
        part = pl.ds(j * REF_PIECE, REF_PIECE)
        props_t[:, part] = properties[part, :].astype(jnp.float32).T.astype(jnp.bfloat16)

    def distribute_aux():
        for t in range(1, STEPS):
            aux_x(t).wait_recv()
        for d in range(1, n_row):
            aux_stage[d] = aux_in[visit_of(d)]
            aux_to_z(d).start()
        aux_z[0] = aux_in[visit_of(0)]

    def distribute(c):
        for t in range(STEPS):
            skew = ref_skew[lax.rem(place + t, n_pb)]
            block = gathered[c][lax.rem(slot + skew + t, n_row)]
            if t == 0:
                queries_in[c][0] = block
            else:
                queries_stage[c][t] = block
                go_x(c, t).start()

    def attend(c, d):
        queries = queries_in[c][visit_of(d)]
        columns = slice(c * rows, (c + 1) * rows)
        sharpen = aux_z[d, 0:1, columns]
        own_sq = aux_z[d, 1:2, columns]
        top = jnp.full((1, rows), LOW, jnp.float32)
        for j in range(ref_tiles):
            part = slice(j * tile_rows, (j + 1) * tile_rows)
            inner = lax.dot_general(
                refs[part, :], queries, NT, preferred_element_type=jnp.float32
            )
            score = sharpen * inner / (ref_sq[part, :] + own_sq - inner)
            score = score + aux_z[d, 2 + j : 3 + j, columns]
            scores[part, :] = score
            top = jnp.maximum(top, jnp.max(score, axis=0, keepdims=True))
        total = jnp.zeros((1, rows), jnp.float32)
        weighted = jnp.zeros((prop_width, rows), jnp.float32)
        for j in range(ref_tiles):
            part = slice(j * tile_rows, (j + 1) * tile_rows)
            weights = jnp.exp(scores[part, :] - top)
            total = total + jnp.sum(weights, axis=0, keepdims=True)
            weighted = weighted + jnp.dot(
                props_t[:, part], weights.astype(jnp.bfloat16), preferred_element_type=jnp.float32
            )
        stats = split_three(top) + split_three(total)
        stats.append(jnp.zeros((STAT_ROWS - len(stats), rows), jnp.float32))
        return weighted.astype(jnp.bfloat16), jnp.concatenate(stats, axis=0).astype(jnp.bfloat16)

    def work(c):
        if c == 0:
            for d in range(1, n_row):
                aux_to_z(d).wait_recv()
        for t in range(1, STEPS):
            go_x(c, t).wait_recv()

        def one(d, _):
            weighted, stats = attend(c, d)
            made[c][d, 0:prop_width, :] = weighted
            made[c][d, prop_width:, :] = stats

            @pl.when(d > 0)
            def _():
                back_z(c, d).start()

            return 0

        lax.fori_loop(0, n_row, one, 0)
        returned[c][0] = made[c][0]

    def collect(c):
        for d in range(1, n_row):
            back_z(c, d).wait_recv()
        for t in range(STEPS - 1, 0, -1):
            passed[c][t] = returned[c][turned(t)]
            back_x(c, t).start()
        finished[c][0] = returned[c][turned(0)]

    def finish(c):
        for t in range(1, STEPS):
            back_x(c, t).wait_recv()
        tops, totals = [], []
        for t in range(STEPS):
            stats = finished[c][t, prop_width:, :].astype(jnp.float32)
            tops.append(stats[0:1] + stats[1:2] + stats[2:3])
            totals.append(stats[3:4] + stats[4:5] + stats[5:6])
        top = functools.reduce(jnp.maximum, tops)
        total = jnp.zeros((1, rows), jnp.float32)
        weighted = jnp.zeros((prop_width, rows), jnp.float32)
        for t in range(STEPS):
            rescale = jnp.exp(tops[t] - top)
            total = total + rescale * totals[t]
            weighted = weighted + rescale * finished[c][t, 0:prop_width, :].astype(jnp.float32)
        out[c * rows : (c + 1) * rows, :] = (weighted / total).T

    for step in range(chunks + n_row + 2):
        for h in range(n_row):
            if 0 <= step - h < chunks and step > 0:
                hop(step - h, h)
        if step == 1:
            distribute_aux()
        for lag, stage in ((0, distribute), (1, work), (2, collect), (3, finish)):
            c = step - (n_row - 1) - lag
            if 0 <= c < chunks:
                stage(c)

    for t in range(1, STEPS):
        aux_x(t).wait_send()
    for d in range(1, n_row):
        aux_to_z(d).wait_send()
    for c in range(chunks):
        for t in range(1, STEPS):
            go_x(c, t).wait_send()
            back_x(c, t).wait_send()
        for d in range(1, n_row):
            back_z(c, d).wait_send()
        for h in range(n_row - 1):
            sent(c, h)


def local(query_emb, query_scales, sharpness, ref_emb, ref_scales, properties, band_mask, ref_skew):
    n_pb = lax.axis_size("pb")
    n_row = lax.axis_size("row")
    query_total, width = query_emb.shape
    ref_total = ref_emb.shape[0]
    prop_width = properties.shape[1]
    rows = query_total // CHUNKS
    low = jnp.bfloat16
    packed = (prop_width + STAT_ROWS, rows)
    kinds = [
        (n_row, rows, width),
        (STEPS, rows, width),
        (STEPS, rows, width),
        (n_row,) + packed,
        (n_row,) + packed,
        (STEPS,) + packed,
        (STEPS,) + packed,
    ]
    vmem = pl.BlockSpec(memory_space=pltpu.VMEM)
    smem = pl.BlockSpec(memory_space=pltpu.SMEM)
    dma = pltpu.SemaphoreType.DMA
    sems = [STEPS, STEPS, n_row, n_row]
    sems += [CHUNKS * STEPS] * 2 + [CHUNKS * n_row] * 6 + [CHUNKS * STEPS] * 2
    pairs = STEPS * query_total * ref_total
    return pl.pallas_call(
        functools.partial(kernel, n_pb, n_row),
        out_shape=jax.ShapeDtypeStruct((query_total, prop_width), jnp.float32),
        in_specs=[vmem] * 6 + [smem] * 2,
        out_specs=vmem,
        scratch_shapes=[
            pltpu.VMEM((ref_total, width), low),
            pltpu.VMEM((ref_total, rows), jnp.float32),
            pltpu.VMEM((prop_width, ref_total), low),
            pltpu.VMEM((ref_total, rows), jnp.float32),
            pltpu.VMEM((STEPS, 8, query_total), jnp.float32),
            pltpu.VMEM((STEPS, 8, query_total), jnp.float32),
            pltpu.VMEM((n_row, 8, query_total), jnp.float32),
            pltpu.VMEM((n_row, 8, query_total), jnp.float32),
        ]
        + [dma((count,)) for count in sems]
        + [pltpu.VMEM(kind, low) for kind in kinds for _ in range(CHUNKS)],
        compiler_params=pltpu.CompilerParams(
            collective_id=0, has_side_effects=True, vmem_limit_bytes=56 * 1024 * 1024
        ),
        cost_estimate=pl.CostEstimate(
            flops=2 * pairs * (width + prop_width),
            bytes_accessed=4 * 1024 * 1024,
            transcendentals=2 * pairs,
        ),
    )(
        query_emb,
        query_scales.T,
        sharpness.reshape(1, query_total),
        ref_emb,
        ref_scales.T,
        properties,
        band_mask,
        ref_skew,
    )


def solution(mesh):
    placed = (
        P(("pb", "row"), None),
        P(("pb", "row"), None),
        P(("pb", "row")),
        P(("pb", "row"), None),
        P(("pb", "row"), None),
        P(("pb", "row"), None),
        P(("pb", "row"), None),
        P(),
    )
    return jax.shard_map(
        local, mesh=mesh, in_specs=placed, out_specs=P(("pb", "row"), None), check_vma=False
    )
```

```python
import functools

import jax
import jax.numpy as jnp
from jax import lax
from jax.experimental import pallas as pl
from jax.experimental.pallas import tpu as pltpu
from jax.sharding import PartitionSpec as P

STEPS = 4
CHUNKS = 4
REF_PIECE = 256
STAT_ROWS = 16
EPSILON = 1e-06
FLOOR = -1e30
LOW = -1e29
MESH = pl.DeviceIdType.MESH
NT = (((1,), (1,)), ((), ()))


def dequantize(values, scales):
    groups = scales.shape[0]
    scales = jnp.concatenate([scales, jnp.zeros((8 - groups, scales.shape[1]), jnp.float32)], axis=0).T
    width = values.shape[1] // groups
    wide = values.astype(jnp.float32)
    parts = [
        (wide[:, g * width : (g + 1) * width] * scales[:, g : g + 1]).astype(jnp.bfloat16)
        for g in range(groups)
    ]
    return jnp.concatenate(parts, axis=1)


def split_squares(matrix):
    square = jnp.square(matrix.astype(jnp.float32))
    high = square.astype(jnp.bfloat16)
    return high, (square - high.astype(jnp.float32)).astype(jnp.bfloat16)


def split_three(value):
    high = value.astype(jnp.bfloat16).astype(jnp.float32)
    rest = value - high
    middle = rest.astype(jnp.bfloat16).astype(jnp.float32)
    return [high, middle, rest - middle]


def kernel(
    n_pb,
    n_row,
    query_emb,
    query_scales,
    sharpness,
    ref_emb,
    ref_scales,
    properties,
    band_mask,
    ref_skew,
    out,
    refs,
    ref_sq,
    props_t,
    scores,
    aux_own,
    aux_in,
    aux_stage,
    aux_z,
    aux_x_send,
    aux_x_recv,
    aux_z_send,
    aux_z_recv,
    x_send,
    x_recv,
    up_send,
    up_recv,
    down_send,
    down_recv,
    rz_send,
    rz_recv,
    rx_send,
    rx_recv,
    *buffers,
):
    place = lax.axis_index("pb")
    slot = lax.axis_index("row")
    chunks = CHUNKS
    gathered = buffers[0:chunks]
    queries_stage = buffers[chunks : 2 * chunks]
    queries_in = buffers[2 * chunks : 3 * chunks]
    made = buffers[3 * chunks : 4 * chunks]
    returned = buffers[4 * chunks : 5 * chunks]
    passed = buffers[5 * chunks : 6 * chunks]
    finished = buffers[6 * chunks : 7 * chunks]

    query_total, width = query_emb.shape
    ref_total = ref_emb.shape[0]
    rows = query_total // chunks
    tile_rows = query_total // band_mask.shape[0]
    query_tiles = query_total // tile_rows
    ref_tiles = ref_total // tile_rows
    prop_width = properties.shape[1]

    def at_pb(steps):
        return (lax.rem(place + n_pb + steps, n_pb), slot)

    def at_row(steps):
        return (place, lax.rem(slot + n_row + steps, n_row))

    partners = [at_pb(t) for t in range(1, STEPS)] + [at_pb(-t) for t in range(1, STEPS)]
    partners += [at_row(d) for d in range(1, n_row)]
    barrier = pltpu.get_barrier_semaphore()
    for partner in partners:
        pl.semaphore_signal(barrier, inc=1, device_id=partner, device_id_type=MESH)

    def remote(source, target, send, recv, device):
        return pltpu.make_async_remote_copy(
            src_ref=source,
            dst_ref=target,
            send_sem=send,
            recv_sem=recv,
            device_id=device,
            device_id_type=MESH,
        )

    def aux_x(t):
        return remote(
            aux_own.at[t], aux_in.at[t], aux_x_send.at[t], aux_x_recv.at[t], at_pb(t)
        )

    def aux_to_z(d):
        return remote(
            aux_stage.at[d], aux_z.at[d], aux_z_send.at[d], aux_z_recv.at[d], at_row(d)
        )

    def go_x(c, t):
        k = c * STEPS + t
        return remote(
            queries_stage[c].at[t], queries_in[c].at[t], x_send.at[k], x_recv.at[k], at_pb(t)
        )

    def go_up(c, h):
        block = gathered[c].at[lax.rem(slot + n_row - h, n_row)]
        k = c * n_row + h
        return remote(block, block, up_send.at[k], up_recv.at[k], at_row(1))

    def go_down(c, h):
        block = gathered[c].at[lax.rem(slot + h, n_row)]
        k = c * n_row + h
        return remote(block, block, down_send.at[k], down_recv.at[k], at_row(-1))

    def from_below(c, h):
        block = gathered[c].at[lax.rem(slot + n_row - h, n_row)]
        k = c * n_row + h - 1
        return remote(block, block, up_send.at[k], up_recv.at[k], at_row(1))

    def from_above(c, h):
        block = gathered[c].at[lax.rem(slot + h, n_row)]
        k = c * n_row + h - 1
        return remote(block, block, down_send.at[k], down_recv.at[k], at_row(-1))

    def hop(c, h):
        @pl.when(slot >= h)
        def _():
            if h > 0:
                from_below(c, h).wait_recv()

            @pl.when(slot < n_row - 1)
            def _():
                go_up(c, h).start()

        @pl.when(slot + h < n_row)
        def _():
            if h > 0:
                from_above(c, h).wait_recv()

            @pl.when(slot > 0)
            def _():
                go_down(c, h).start()

    def sent(c, h):
        @pl.when((slot >= h) & (slot < n_row - 1))
        def _():
            go_up(c, h).wait_send()

        @pl.when((slot + h < n_row) & (slot > 0))
        def _():
            go_down(c, h).wait_send()

    def back_z(c, d):
        k = c * n_row + d
        return remote(
            made[c].at[d], returned[c].at[d], rz_send.at[k], rz_recv.at[k], at_row(-d)
        )

    def back_x(c, t):
        k = c * STEPS + t
        return remote(
            passed[c].at[t], finished[c].at[t], rx_send.at[k], rx_recv.at[k], at_pb(-t)
        )

    own_skew = ref_skew[place]

    def turned(steps):
        return lax.rem(2 * n_row - steps - own_skew, n_row)

    def visit_of(d):
        return jnp.minimum(turned(d), STEPS - 1)

    ones_ref = jnp.ones((rows, width), jnp.bfloat16)

    def prepare(i, _):
        part = pl.ds(pl.multiple_of(i * REF_PIECE, REF_PIECE), REF_PIECE)
        block = dequantize(ref_emb[part, :], ref_scales[:, part])
        refs[part, :] = block
        high, low = split_squares(block)
        ref_sq[part, :] = (
            lax.dot_general(high, ones_ref, NT, preferred_element_type=jnp.float32)
            + lax.dot_general(low, ones_ref, NT, preferred_element_type=jnp.float32)
            + EPSILON
        )
        return 0

    lax.fori_loop(0, ref_total // REF_PIECE, prepare, 0)
    for j in range(ref_total // REF_PIECE):
        part = pl.ds(j * REF_PIECE, REF_PIECE)
        props_t[:, part] = properties[part, :].astype(jnp.float32).T.astype(jnp.bfloat16)

    ones = jnp.ones((8, width), jnp.bfloat16)
    for c in range(chunks):
        part = pl.ds(c * rows, rows)
        gathered[c][slot] = dequantize(query_emb[part, :], query_scales[:, part])
        if c == 0:
            pl.semaphore_wait(barrier, len(partners))
            hop(0, 0)
    lanes = lax.broadcasted_iota(jnp.int32, (1, query_total), 1) // tile_rows
    squares = []
    for c in range(chunks):
        high, low = split_squares(gathered[c][slot])
        squares.append(
            (
                lax.dot_general(ones, high, NT, preferred_element_type=jnp.float32)
                + lax.dot_general(ones, low, NT, preferred_element_type=jnp.float32)
            )[0:1]
        )
    query_sq = jnp.concatenate(squares, axis=1)
    for t in range(STEPS):
        group = lax.rem(place + t, n_pb)
        row_slot = lax.rem(slot - ref_skew[group] - t + 8 * n_row, n_row)
        first = (group * n_row + row_slot) * ref_tiles
        lines = [sharpness[...], query_sq]
        for j in range(ref_tiles):
            line = jnp.zeros((1, query_total), jnp.float32)
            for i in range(query_tiles):
                bias = jnp.where(band_mask[i, first + j] == 1, 0.0, FLOOR)
                line = jnp.where(lanes == i, bias, line)
            lines.append(line)
        lines.append(jnp.zeros((8 - len(lines), query_total), jnp.float32))
        (aux_in.at[0] if t == 0 else aux_own.at[t])[...] = jnp.concatenate(lines, axis=0)
        if t > 0:
            aux_x(t).start()

    def distribute_aux():
        for t in range(1, STEPS):
            aux_x(t).wait_recv()
        for d in range(1, n_row):
            aux_stage[d] = aux_in[visit_of(d)]
            aux_to_z(d).start()
        aux_z[0] = aux_in[visit_of(0)]

    def distribute(c):
        for t in range(STEPS):
            skew = ref_skew[lax.rem(place + t, n_pb)]
            block = gathered[c][lax.rem(slot + skew + t, n_row)]
            if t == 0:
                queries_in[c][0] = block
            else:
                queries_stage[c][t] = block
                go_x(c, t).start()

    def attend(c, d):
        queries = queries_in[c][visit_of(d)]
        columns = slice(c * rows, (c + 1) * rows)
        sharpen = aux_z[d, 0:1, columns]
        own_sq = aux_z[d, 1:2, columns]
        top = jnp.full((1, rows), LOW, jnp.float32)
        for j in range(ref_tiles):
            part = slice(j * tile_rows, (j + 1) * tile_rows)
            inner = lax.dot_general(
                refs[part, :], queries, NT, preferred_element_type=jnp.float32
            )
            score = sharpen * inner / (ref_sq[part, :] + own_sq - inner)
            score = score + aux_z[d, 2 + j : 3 + j, columns]
            scores[part, :] = score
            top = jnp.maximum(top, jnp.max(score, axis=0, keepdims=True))
        total = jnp.zeros((1, rows), jnp.float32)
        weighted = jnp.zeros((prop_width, rows), jnp.float32)
        for j in range(ref_tiles):
            part = slice(j * tile_rows, (j + 1) * tile_rows)
            weights = jnp.exp(scores[part, :] - top)
            total = total + jnp.sum(weights, axis=0, keepdims=True)
            weighted = weighted + jnp.dot(
                props_t[:, part], weights.astype(jnp.bfloat16), preferred_element_type=jnp.float32
            )
        stats = split_three(top) + split_three(total)
        stats.append(jnp.zeros((STAT_ROWS - len(stats), rows), jnp.float32))
        return weighted.astype(jnp.bfloat16), jnp.concatenate(stats, axis=0).astype(jnp.bfloat16)

    def work(c):
        if c == 0:
            for d in range(1, n_row):
                aux_to_z(d).wait_recv()
        for t in range(1, STEPS):
            go_x(c, t).wait_recv()

        def one(d, _):
            weighted, stats = attend(c, d)
            made[c][d, 0:prop_width, :] = weighted
            made[c][d, prop_width:, :] = stats

            @pl.when(d > 0)
            def _():
                back_z(c, d).start()

            return 0

        lax.fori_loop(0, n_row, one, 0)
        returned[c][0] = made[c][0]

    def collect(c):
        for d in range(1, n_row):
            back_z(c, d).wait_recv()
        for t in range(STEPS - 1, 0, -1):
            passed[c][t] = returned[c][turned(t)]
            back_x(c, t).start()
        finished[c][0] = returned[c][turned(0)]

    def finish(c):
        for t in range(1, STEPS):
            back_x(c, t).wait_recv()
        tops, totals = [], []
        for t in range(STEPS):
            stats = finished[c][t, prop_width:, :].astype(jnp.float32)
            tops.append(stats[0:1] + stats[1:2] + stats[2:3])
            totals.append(stats[3:4] + stats[4:5] + stats[5:6])
        top = functools.reduce(jnp.maximum, tops)
        total = jnp.zeros((1, rows), jnp.float32)
        weighted = jnp.zeros((prop_width, rows), jnp.float32)
        for t in range(STEPS):
            rescale = jnp.exp(tops[t] - top)
            total = total + rescale * totals[t]
            weighted = weighted + rescale * finished[c][t, 0:prop_width, :].astype(jnp.float32)
        out[c * rows : (c + 1) * rows, :] = (weighted / total).T

    for step in range(chunks + n_row + 2):
        for h in range(n_row):
            if 0 <= step - h < chunks and step > 0:
                hop(step - h, h)
        if step == 1:
            distribute_aux()
        for lag, stage in ((0, distribute), (1, work), (2, collect), (3, finish)):
            c = step - (n_row - 1) - lag
            if 0 <= c < chunks:
                stage(c)

    for t in range(1, STEPS):
        aux_x(t).wait_send()
    for d in range(1, n_row):
        aux_to_z(d).wait_send()
    for c in range(chunks):
        for t in range(1, STEPS):
            go_x(c, t).wait_send()
            back_x(c, t).wait_send()
        for d in range(1, n_row):
            back_z(c, d).wait_send()
        for h in range(n_row - 1):
            sent(c, h)


def local(query_emb, query_scales, sharpness, ref_emb, ref_scales, properties, band_mask, ref_skew):
    n_pb = lax.axis_size("pb")
    n_row = lax.axis_size("row")
    query_total, width = query_emb.shape
    ref_total = ref_emb.shape[0]
    prop_width = properties.shape[1]
    rows = query_total // CHUNKS
    low = jnp.bfloat16
    packed = (prop_width + STAT_ROWS, rows)
    kinds = [
        (n_row, rows, width),
        (STEPS, rows, width),
        (STEPS, rows, width),
        (n_row,) + packed,
        (n_row,) + packed,
        (STEPS,) + packed,
        (STEPS,) + packed,
    ]
    vmem = pl.BlockSpec(memory_space=pltpu.VMEM)
    smem = pl.BlockSpec(memory_space=pltpu.SMEM)
    dma = pltpu.SemaphoreType.DMA
    sems = [STEPS, STEPS, n_row, n_row]
    sems += [CHUNKS * STEPS] * 2 + [CHUNKS * n_row] * 6 + [CHUNKS * STEPS] * 2
    pairs = STEPS * query_total * ref_total
    return pl.pallas_call(
        functools.partial(kernel, n_pb, n_row),
        out_shape=jax.ShapeDtypeStruct((query_total, prop_width), jnp.float32),
        in_specs=[vmem] * 6 + [smem] * 2,
        out_specs=vmem,
        scratch_shapes=[
            pltpu.VMEM((ref_total, width), low),
            pltpu.VMEM((ref_total, rows), jnp.float32),
            pltpu.VMEM((prop_width, ref_total), low),
            pltpu.VMEM((ref_total, rows), jnp.float32),
            pltpu.VMEM((STEPS, 8, query_total), jnp.float32),
            pltpu.VMEM((STEPS, 8, query_total), jnp.float32),
            pltpu.VMEM((n_row, 8, query_total), jnp.float32),
            pltpu.VMEM((n_row, 8, query_total), jnp.float32),
        ]
        + [dma((count,)) for count in sems]
        + [pltpu.VMEM(kind, low) for kind in kinds for _ in range(CHUNKS)],
        compiler_params=pltpu.CompilerParams(
            collective_id=0, has_side_effects=True, vmem_limit_bytes=56 * 1024 * 1024
        ),
        cost_estimate=pl.CostEstimate(
            flops=2 * pairs * (width + prop_width),
            bytes_accessed=4 * 1024 * 1024,
            transcendentals=2 * pairs,
        ),
    )(
        query_emb,
        query_scales.T,
        sharpness.reshape(1, query_total),
        ref_emb,
        ref_scales.T,
        properties,
        band_mask,
        ref_skew,
    )


def solution(mesh):
    placed = (
        P(("pb", "row"), None),
        P(("pb", "row"), None),
        P(("pb", "row")),
        P(("pb", "row"), None),
        P(("pb", "row"), None),
        P(("pb", "row"), None),
        P(("pb", "row"), None),
        P(),
    )
    return jax.shard_map(
        local, mesh=mesh, in_specs=placed, out_specs=P(("pb", "row"), None), check_vma=False
    )
```
